512 devices in a mesh: row: 64 (over z_lo, y, core), col: 8 (over z_hi, x).
Axes of the slice: x: 4, y: 8, z: 8 (z_hi: 2, z_lo: 4; z = z_hi * 4 + z_lo), core: 2. Of those that a mesh axis runs over, the one named last changes fastest.
Arguments:
- homolog_activations: bfloat16 [1024, 64, 256], P(('row', 'col')), may hold values from -6 to 6
- first_linear_matrix: bfloat16 [256, 32], replicated, may hold values from -0.375 to 0.375
- second_linear_matrix: bfloat16 [256, 32], replicated, may hold values from -0.375 to 0.375
- output_weight: bfloat16 [1024, 128], replicated, may hold values from -0.1875 to 0.1875
- output_bias: float32 [128], replicated, may hold values from -3 to 3
- pair_update_gradient: bfloat16 [1024, 1024, 128], P('row', 'col'), may hold values from -6 to 6
Outputs:
- pair_representation_update: bfloat16 [1024, 1024, 128], P('row', 'col')
- activation_sensitivity: bfloat16 [1024, 64, 256], P(('row', 'col'))
- output_weight_gradient: float32 [1024, 128], replicated
The draws below stay inside these ranges and needn't reach their ends.
All inputs are finite; a program needn't handle non-finite values.
Results may differ from the reference program's by a relative error of at most 0.015.
Values may be sent and summed in bfloat16 or wider, within the bound.
A program may use at most 64 MiB of HBM per device.

```python
import jax
import jax.numpy as jnp
from jax import lax

FEATURE_LENGTH = 256
HIDDEN_FEATURES = 32
C_Z = 128
HOMOLOG_NUMBER = 64
RES_ROW = 16
AMINO_TOTAL = 1024
N_ROW = 64


def block_levels(rng, extent, shards, smallest, top_value):
    def one(position, parts):
        steps = jax.random.uniform(jax.random.fold_in(jax.random.fold_in(rng, 6), position), (parts,), jnp.float32, smallest / len(shards), top_value / len(shards))
        return jnp.repeat(jnp.exp(steps), extent[position] // parts).reshape((-1,) + (1,) * (len(extent) - position - 1))

    loudness = one(*shards[0])
    for cut in shards[1:]:
        loudness = loudness * one(*cut)
    return loudness


def bell_draw(key, shape, deviation, limit, cuts=(), dtype=jnp.bfloat16):
    array = deviation * jax.random.normal(key, shape, jnp.float32)
    if cuts:
        array = array * block_levels(key, shape, cuts, -0.22, 0.18)
    return jnp.clip(array, -limit, limit).astype(dtype)


def setup_inputs(seed: int = 0) -> dict:
    keys = jax.random.split(jax.random.key(seed), 7)
    return {
        "homolog_activations": bell_draw(keys[0], (AMINO_TOTAL, HOMOLOG_NUMBER, FEATURE_LENGTH), 1.0, 6.0, ((0, 512),)),
        "first_linear_matrix": bell_draw(keys[1], (FEATURE_LENGTH, HIDDEN_FEATURES), FEATURE_LENGTH ** -0.5, 0.375),
        "second_linear_matrix": bell_draw(keys[2], (FEATURE_LENGTH, HIDDEN_FEATURES), FEATURE_LENGTH ** -0.5, 0.375),
        "output_weight": bell_draw(keys[3], (HIDDEN_FEATURES * HIDDEN_FEATURES, C_Z), (HIDDEN_FEATURES * HIDDEN_FEATURES) ** -0.5, 0.1875),
        "output_bias": bell_draw(keys[4], (C_Z,), 0.5, 3.0, (), jnp.float32),
        "pair_update_gradient": bell_draw(keys[5], (AMINO_TOTAL, AMINO_TOTAL, C_Z), 1.0, 6.0, ((0, 64), (1, 8))),
    }


EPSILON = 1e-05

def layer_normalize(homolog_activations):
    value_entries = homolog_activations.astype(jnp.float32)
    center = lax.optimization_barrier(jnp.mean(value_entries, axis=-1, keepdims=True))
    spread = lax.optimization_barrier(jnp.mean(jnp.square(value_entries - center), axis=-1, keepdims=True))
    reciprocal_spread_factor = lax.rsqrt(spread + EPSILON)
    return ((value_entries - center) * reciprocal_spread_factor, reciprocal_spread_factor)

def project(normed, weight):
    flat_rows = normed.reshape(-1, normed.shape[-1])
    result = jnp.dot(flat_rows, weight, preferred_element_type=jnp.float32).astype(jnp.bfloat16)
    return result.reshape(normed.shape[0], normed.shape[1], weight.shape[1])

def standardizer_adjoint(standardized_sensitivity, rescaled_features, reciprocal_spread_factor):
    mean_grad = lax.optimization_barrier(jnp.mean(standardized_sensitivity, axis=-1, keepdims=True))
    mean_cross = lax.optimization_barrier(jnp.mean(standardized_sensitivity * rescaled_features, axis=-1, keepdims=True))
    return (reciprocal_spread_factor * (standardized_sensitivity - mean_grad - rescaled_features * mean_cross)).astype(jnp.bfloat16)

def reference(homolog_activations, first_linear_matrix, second_linear_matrix, output_weight, output_bias, pair_update_gradient):
    rescaled_features, reciprocal_spread_factor = layer_normalize(homolog_activations)
    normed = rescaled_features.astype(jnp.bfloat16)
    left = project(normed, first_linear_matrix)
    right = project(normed, second_linear_matrix)
    right_full = right.astype(jnp.float32)
    left_blocks = left.reshape(N_ROW, RES_ROW, HOMOLOG_NUMBER, HIDDEN_FEATURES)
    grad_blocks = pair_update_gradient.reshape(N_ROW, RES_ROW, AMINO_TOTAL, C_Z)

    def step(carry, inputs):
        weight_acc, right_acc = carry
        left_tile_block, grad_block = inputs
        left_full = left_tile_block.astype(jnp.float32)
        outer = jnp.einsum('isc,jse->ijce', left_full, right_full) / HOMOLOG_NUMBER
        outer = outer.astype(jnp.bfloat16).reshape(-1, HIDDEN_FEATURES * HIDDEN_FEATURES)
        pair_block = (jnp.dot(outer, output_weight, preferred_element_type=jnp.float32) + output_bias).astype(jnp.bfloat16)
        cotangent = grad_block.reshape(-1, C_Z)
        grad_outer = jnp.dot(cotangent, output_weight.T, preferred_element_type=jnp.float32).astype(jnp.bfloat16)
        weight_acc = weight_acc + jnp.dot(outer.T, cotangent, preferred_element_type=jnp.float32)
        grad_four = grad_outer.astype(jnp.float32).reshape(RES_ROW, AMINO_TOTAL, HIDDEN_FEATURES, HIDDEN_FEATURES)
        grad_left = jnp.einsum('ijce,jse->isc', grad_four, right_full) / HOMOLOG_NUMBER
        right_acc = right_acc + jnp.einsum('ijce,isc->jse', grad_four, left_full) / HOMOLOG_NUMBER
        return ((weight_acc, right_acc), (pair_block.reshape(RES_ROW, AMINO_TOTAL, C_Z), grad_left))
    start = (jnp.zeros((HIDDEN_FEATURES * HIDDEN_FEATURES, C_Z), jnp.float32), jnp.zeros((AMINO_TOTAL, HOMOLOG_NUMBER, HIDDEN_FEATURES), jnp.float32))
    (weight_acc, grad_right), (pair_blocks, grad_left) = lax.scan(step, start, (left_blocks, grad_blocks))
    pair_representation_update = pair_blocks.reshape(AMINO_TOTAL, AMINO_TOTAL, C_Z)
    grad_left = grad_left.reshape(AMINO_TOTAL * HOMOLOG_NUMBER, HIDDEN_FEATURES)
    grad_right = grad_right.reshape(AMINO_TOTAL * HOMOLOG_NUMBER, HIDDEN_FEATURES)
    standardized_sensitivity = jnp.dot(grad_left, first_linear_matrix.astype(jnp.float32).T, precision=lax.Precision.HIGHEST)
    standardized_sensitivity = standardized_sensitivity + jnp.dot(grad_right, second_linear_matrix.astype(jnp.float32).T, precision=lax.Precision.HIGHEST)
    activation_sensitivity = standardizer_adjoint(standardized_sensitivity.reshape(AMINO_TOTAL, HOMOLOG_NUMBER, FEATURE_LENGTH), rescaled_features, reciprocal_spread_factor)
    output_weight_gradient = weight_acc * (8.0 / AMINO_TOTAL)
    return (pair_representation_update, activation_sensitivity, output_weight_gradient)
```

```python
import functools

import jax
import jax.numpy as jnp
from jax import lax
from jax.experimental import pallas as pl
from jax.experimental.pallas import tpu as pltpu
from jax.sharding import PartitionSpec as P

EPSILON = 1e-05
MESH = pl.DeviceIdType.MESH
BF = jnp.bfloat16
F32 = jnp.float32


def f32dot(a, b, dims):
    return lax.dot_general(a, b, (dims, ((), ())), preferred_element_type=F32)


def kernel(
    acts, w1, w2, w_hbm, bias, g_hbm,
    pair_hbm, sens, wg_out,
    scaled_v, inv_v, wcat, wbuf, wf, wc, gcat, lbuf, lm, ltc, xr, rraw, rf, r2d, rt,
    tmat, umat, grb, grx, gf, grs, gry, grz, gro, gls, glr,
    wg32, wgb, wgx, whb, wy, wzb, wxb, wfin, pbuf,
    s_loc, s_g, s_p, l_s, l_r, a_s, a_r, b_s, b_r, c_s, c_r, x_s, x_r, y_s, y_r, o_s, o_r, gl_s, gl_r,
    w0_s, w0_r, w1_s, w1_r, w2_s, w2_r, w3_s, w3_r, w4_s, w4_r, w5_s, w5_r,
):
    row = lax.axis_index("row")
    col = lax.axis_index("col")
    zl, y, k = row // 16, (row // 2) % 8, row % 2
    zh, x = col // 4, col % 4
    z = zh * 4 + zl
    other = 1 - k
    cy = (2 * y + 1) % 9
    home = row // 8
    fy = (5 * col + 4) % 9
    mq = (row % 8) // 2

    def row_of(a, b, c):
        return a * 16 + b * 2 + c

    y_peers = [(row_of(zl, (y + d) % 8, k), col) for d in range(1, 8)]
    col_peers = [(row, (col + d) % 8) for d in range(1, 8)]
    x_peers = [(row, zh * 4 + (x + d) % 4) for d in range(1, 4)]
    z_peers = [
        (row_of(((z + d) % 8) % 4, y, k), (((z + d) % 8) // 4) * 4 + x) for d in range(1, 8)
    ]
    twin = (row_of(zl, y, other), col)
    takers = [(row_of(a, fy, k), home) for a in range(4)]
    owners = [(8 * col + 2 * m + k, cy) for m in range(4)]

    def send(src, dst, ss, rs, dev):
        cp = pltpu.make_async_remote_copy(
            src_ref=src, dst_ref=dst, send_sem=ss, recv_sem=rs, device_id=dev, device_id_type=MESH
        )
        cp.start()
        return cp

    loads = [pltpu.make_async_copy(w_hbm, wbuf, s_loc.at[0])]
    loads[0].start()
    gloads = []
    for i in range(16):
        cp = pltpu.make_async_copy(g_hbm.at[i], gcat.at[:, pl.ds(i * 128, 128)], s_g.at[i])
        cp.start()
        gloads.append(cp)

    barrier = pltpu.get_barrier_semaphore()
    greet = y_peers + col_peers + z_peers + [twin] + takers + owners
    for dev in greet:
        pl.semaphore_signal(barrier, inc=1, device_id=dev, device_id_type=MESH)

    wcat[...] = jnp.concatenate([w1[...], w2[...], jnp.zeros((256, 64), BF)], axis=1)
    xv = acts[...].astype(F32).reshape(128, 256)
    center = jnp.mean(xv, axis=-1, keepdims=True)
    diff = xv - center
    inv = lax.rsqrt(jnp.mean(diff * diff, axis=-1, keepdims=True) + EPSILON)
    scaled = diff * inv
    scaled_v[...] = scaled
    inv_v[...] = inv
    proj = f32dot(scaled.astype(BF), wcat[...], ((1,), (0,)))
    projt = proj.T
    low = lax.broadcasted_iota(jnp.int32, (16, 128), 1) < 64
    lbuf[col] = projt[0:32].astype(BF)
    ra, rb = projt[32:48], projt[48:64]
    xr[0:16] = jnp.where(low, ra, pltpu.roll(rb, 64, 1)).astype(BF)
    xr[16:32] = jnp.where(low, pltpu.roll(ra, 64, 1), rb).astype(BF)

    pl.semaphore_wait(barrier, len(greet))

    sent = []
    l_cp = [
        send(lbuf.at[col], lbuf.at[col], l_s.at[d], l_r.at[d], col_peers[d]) for d in range(7)
    ]
    a_cp = [
        send(xr, rraw.at[mq, k, col], a_s.at[a], a_r.at[mq], takers[a]) for a in range(4)
    ]
    sent += l_cp + a_cp

    loads[0].wait()
    wf[...] = wbuf[...].astype(F32)
    for e in range(32):
        pos = (e % 16) * 2 + e // 16
        wc[:, pos * 128:(pos + 1) * 128] = wf[pl.ds(e, 32, stride=32), :].astype(BF)

    for cp in l_cp:
        cp.wait_recv()
    for c in range(8):
        blk = lbuf[c]
        ltc[:, c * 128:(c + 1) * 128] = blk
        lm[c * 128:(c + 1) * 128, :] = blk.astype(F32).T.astype(BF)

    for m in range(4):
        pltpu.make_async_remote_copy(
            src_ref=xr, dst_ref=rraw.at[m, k, cy], send_sem=a_s.at[m], recv_sem=a_r.at[m],
            device_id=twin, device_id_type=MESH,
        ).wait_recv()
    b_cp = [
        send(rraw.at[:, k, cy], rraw.at[:, k, cy], b_s.at[d], b_r.at[d], y_peers[d])
        for d in range(7)
    ]
    c_cp = [send(rraw.at[:, k, cy], rraw.at[:, k, cy], c_s.at[0], c_r.at[0], twin)]
    sent += b_cp

    def t_step(n, _):
        t, ib = n // 4, n % 4
        r0 = pl.multiple_of(ib * 256, 256)
        c0 = pl.multiple_of(t * 256, 256)
        res = f32dot(lm[pl.ds(r0, 256), :], wc[:, pl.ds(c0, 256)], ((1,), (0,))) * (1.0 / 64.0)
        res = res.astype(BF)
        for i in range(4):
            for h in range(2):
                tmat[
                    pl.ds(pl.multiple_of(t * 128 + h * 64, 64), 64),
                    pl.ds(pl.multiple_of(ib * 512 + i * 128, 128), 128),
                ] = res[i * 64:(i + 1) * 64, h * 128:(h + 1) * 128]
        return 0

    lax.fori_loop(0, 64, t_step, 0)

    for cp in gloads:
        cp.wait()

    def gr_step(n, _):
        res = f32dot(gcat[...], tmat[pl.ds(pl.multiple_of(n * 256, 256), 256), :], ((1,), (1,)))
        res = res.astype(BF)
        for tt in range(2):
            for q in range(8):
                grb[q % 2, n * 2 + tt, (q // 2) * 16:(q // 2 + 1) * 16, :] = res[
                    q * 16:(q + 1) * 16, tt * 128:(tt + 1) * 128
                ]
        return 0

    lax.fori_loop(0, 8, gr_step, 0)
    x_cp = send(grb.at[other], grx, x_s, x_r, twin)
    sent.append(x_cp)

    for d in range(7):
        b_cp[d].wait_recv()
        cs = (2 * ((y + 7 - d) % 8) + 1) % 9
        c_cp.append(
            send(rraw.at[:, k, cs], rraw.at[:, k, cs], c_s.at[d + 1], c_r.at[d + 1], twin)
        )
    sent += c_cp

    x_cp.wait_recv()

    def gs_step(t, _):
        gf[pl.ds(t, 64, stride=16), :] = grb[k, t].astype(F32) + grx[t].astype(F32)
        return 0

    lax.fori_loop(0, 16, gs_step, 0)

    def gp_step(m, _):
        blk = gf[pl.ds(pl.multiple_of(m * 256, 256), 256), :].astype(BF)
        grs[m] = blk.reshape(8, 32, 128)
        return 0

    lax.fori_loop(0, 4, gp_step, 0)
    y_cp = []
    for d in range(7):
        cs = (2 * ((y + d + 1) % 8) + 1) % 9
        y_cp.append(send(grs.at[:, cs], gry.at[d], y_s.at[d], y_r.at[d], y_peers[d]))
    sent += y_cp

    for cp in c_cp:
        cp.wait_recv()

    def rf_step(n, _):
        blk = rraw[n // 2, n % 2].reshape(256, 128)
        rf[pl.ds(pl.multiple_of(n * 256, 256), 256), :] = blk.astype(F32)
        return 0

    lax.fori_loop(0, 8, rf_step, 0)

    def rt_step(t, _):
        blk = rf[pl.ds(t, 128, stride=16), :]
        t0 = pl.multiple_of(t * 128, 128)
        r2d[:, pl.ds(t0, 128)] = blk.astype(BF)
        rt[pl.ds(t0, 128), :] = blk.T.astype(BF)
        return 0

    lax.fori_loop(0, 16, rt_step, 0)

    def u_step(t, _):
        t0 = pl.multiple_of(t * 128, 128)
        lhs = rt[pl.ds(t0, 128), :]
        for ib in range(4):
            res = f32dot(lhs, gcat[:, ib * 512:(ib + 1) * 512], ((1,), (0,))).astype(BF)
            for i in range(4):
                for h in range(2):
                    umat[
                        (ib * 4 + i) * 64:(ib * 4 + i + 1) * 64,
                        pl.ds(pl.multiple_of(t * 256 + h * 128, 128), 128),
                    ] = res[h * 64:(h + 1) * 64, i * 128:(i + 1) * 128]
        wt = f32dot(ltc[...], umat[:, pl.ds(pl.multiple_of(t * 256, 256), 256)], ((1,), (0,)))
        for h in range(2):
            part = wt[:, h * 128:(h + 1) * 128]
            r0 = pl.multiple_of(t * 32, 32)
            wg32[h, pl.ds(r0, 32), :] = part
            wgb[h, pl.ds(r0, 32), :] = part.astype(BF)
        return 0

    lax.fori_loop(0, 16, u_step, 0)

    w0_cp = send(wgb.at[other], wgx, w0_s, w0_r, twin)
    sent.append(w0_cp)
    w0_cp.wait_recv()
    for n in range(8):
        whb[n] = (
            wg32[k, n * 64:(n + 1) * 64, :] + wgx[n * 64:(n + 1) * 64, :].astype(F32)
        ).astype(BF)
    w1_cp = [
        send(whb.at[(y + d + 1) % 8], wy.at[d], w1_s.at[d], w1_r.at[d], y_peers[d])
        for d in range(7)
    ]
    sent += w1_cp

    def gl_step(n, _):
        res = f32dot(wc[...], umat[pl.ds(pl.multiple_of(n * 256, 256), 256), :], ((1,), (1,)))
        res = (res * (1.0 / 64.0)).astype(BF)
        gls[n * 2] = res[:, 0:128]
        gls[n * 2 + 1] = res[:, 128:256]
        return 0

    lax.fori_loop(0, 4, gl_step, 0)
    gl_cp = [
        send(gls.at[(col + d + 1) % 8], glr.at[d], gl_s.at[d], gl_r.at[d], col_peers[d])
        for d in range(7)
    ]
    sent += gl_cp

    for cp in y_cp:
        cp.wait_recv()
    for m in range(4):
        acc = grs[m, cy].astype(F32)
        for d in range(7):
            acc = acc + gry[d, m].astype(F32)
        grz[m] = acc.astype(BF)
    o_cp = [send(grz.at[m], gro.at[zl], o_s.at[m], o_r.at[zl], owners[m]) for m in range(4)]
    sent += o_cp

    for cp in w1_cp:
        cp.wait_recv()
    acc = whb[y].astype(F32)
    for d in range(7):
        acc = acc + wy[d].astype(F32)
    wzb[z] = acc.astype(BF)
    w2_cp = [
        send(wzb.at[z], wzb.at[z], w2_s.at[d], w2_r.at[d], z_peers[d]) for d in range(7)
    ]
    sent += w2_cp

    def pair_step(n, _):
        c0 = pl.multiple_of(n * 256, 256)
        res = f32dot(r2d[...], tmat[:, pl.ds(c0, 256)], ((1,), (0,)))
        for i in range(2):
            pbuf[n * 2 + i] = (res[:, i * 128:(i + 1) * 128] + bias[...]).astype(BF)
        return 0

    lax.fori_loop(0, 8, pair_step, 0)
    p_cp = pltpu.make_async_copy(pbuf, pair_hbm, s_p)
    p_cp.start()

    for cp in w2_cp:
        cp.wait_recv()
    acc = wzb[0].astype(F32)
    for n in range(1, 8):
        acc = acc + wzb[n].astype(F32)
    wxb[x] = acc.astype(BF)
    w3_cp = [
        send(wxb.at[x], wxb.at[x], w3_s.at[d], w3_r.at[d], x_peers[d]) for d in range(3)
    ]
    sent += w3_cp
    for cp in w3_cp:
        cp.wait_recv()
    acc = wxb[0].astype(F32)
    for n in range(1, 4):
        acc = acc + wxb[n].astype(F32)
    wfin[k, y] = acc.astype(BF)
    w4_cp = [
        send(wfin.at[k, y], wfin.at[k, y], w4_s.at[d], w4_r.at[d], y_peers[d]) for d in range(7)
    ]
    w5_cp = [send(wfin.at[k, y], wfin.at[k, y], w5_s.at[0], w5_r.at[0], twin)]
    sent += w4_cp

    for cp in gl_cp:
        cp.wait_recv()
    gl = gls[col].astype(F32)
    for d in range(7):
        gl = gl + glr[d].astype(F32)
    for m in range(4):
        pltpu.make_async_remote_copy(
            src_ref=grz.at[m], dst_ref=gro.at[m], send_sem=o_s.at[m], recv_sem=o_r.at[m],
            device_id=twin, device_id_type=MESH,
        ).wait_recv()
    gr = gro[0].astype(F32)
    for m in range(1, 4):
        gr = gr + gro[m].astype(F32)
    x0, x1 = gr[0:16], gr[16:32]
    ga = jnp.where(low, x0, pltpu.roll(x1, 64, 1))
    gb = jnp.where(low, pltpu.roll(x0, 64, 1), x1)
    gt = jnp.concatenate([gl, ga, gb, jnp.zeros((64, 128), F32)], axis=0).T
    hi = gt.astype(BF)
    rest = gt - hi.astype(F32)
    mid = rest.astype(BF)
    lo = (rest - mid.astype(F32)).astype(BF)
    wv = wcat[...]
    nt = ((1,), (1,))
    gn = f32dot(hi, wv, nt) + (f32dot(mid, wv, nt) + f32dot(lo, wv, nt))
    sc = scaled_v[...]
    mean_grad = jnp.mean(gn, axis=-1, keepdims=True)
    mean_cross = jnp.mean(gn * sc, axis=-1, keepdims=True)
    res = inv_v[...] * (gn - mean_grad - sc * mean_cross)
    sens[...] = res.astype(BF).reshape(2, 64, 256)

    for d in range(7):
        w4_cp[d].wait_recv()
        ys = (y + 7 - d) % 8
        w5_cp.append(
            send(wfin.at[k, ys], wfin.at[k, ys], w5_s.at[d + 1], w5_r.at[d + 1], twin)
        )
    sent += w5_cp
    for cp in w5_cp:
        cp.wait_recv()
    for h in range(2):
        for n in range(8):
            blk = wfin[h, n].astype(F32) * (8.0 / 65536.0)
            for tt in range(2):
                e = h * 16 + n * 2 + tt
                wg_out[pl.ds(e, 32, stride=32), :] = blk[tt * 32:(tt + 1) * 32]
    p_cp.wait()
    for cp in sent:
        cp.wait_send()


def on_device(acts, w1, w2, w, bias, g):
    vm = pl.BlockSpec(memory_space=pltpu.VMEM)
    anys = pl.BlockSpec(memory_space=pl.ANY)
    dma = pltpu.SemaphoreType.DMA
    scratch = [
        ((128, 256), F32), ((128, 1), F32), ((256, 128), BF), ((1024, 128), BF), ((1024, 128), F32),
        ((32, 4096), BF), ((128, 2048), BF), ((8, 32, 128), BF), ((1024, 32), BF), ((32, 1024), BF),
        ((32, 128), BF), ((4, 2, 8, 32, 128), BF), ((2048, 128), F32), ((128, 2048), BF),
        ((2048, 128), BF),
        ((2048, 2048), BF), ((1024, 4096), BF), ((2, 16, 64, 128), BF), ((16, 64, 128), BF),
        ((1024, 128), F32), ((4, 8, 32, 128), BF), ((7, 4, 32, 128), BF), ((4, 32, 128), BF),
        ((4, 32, 128), BF), ((8, 32, 128), BF), ((7, 32, 128), BF),
        ((2, 512, 128), F32), ((2, 512, 128), BF), ((512, 128), BF), ((8, 64, 128), BF),
        ((7, 64, 128), BF), ((8, 64, 128), BF), ((4, 64, 128), BF), ((2, 8, 64, 128), BF),
        ((16, 128, 128), BF),
    ]
    scratch = [pltpu.VMEM(s, d) for s, d in scratch]
    scratch += [dma((1,)), dma((16,)), dma]
    for n in (7, 4, 7, 8, 0, 7, 4, 7, 0, 7, 7, 3, 7, 8):
        scratch += [dma((n,)), dma((n,))] if n else [dma, dma]
    return pl.pallas_call(
        kernel,
        out_shape=(
            jax.ShapeDtypeStruct((16, 128, 128), BF),
            jax.ShapeDtypeStruct((2, 64, 256), BF),
            jax.ShapeDtypeStruct((1024, 128), F32),
        ),
        in_specs=[vm, vm, vm, anys, vm, anys],
        out_specs=(anys, vm, vm),
        scratch_shapes=scratch,
        compiler_params=pltpu.CompilerParams(
            collective_id=0, has_side_effects=True, vmem_limit_bytes=48 * 2**20
        ),
    )(acts, w1, w2, w, bias.reshape(1, 128), g)


def solution(mesh):
    return jax.shard_map(
        on_device,
        mesh=mesh,
        in_specs=(P(("row", "col"), None, None), P(), P(), P(), P(), P("row", "col", None)),
        out_specs=(P("row", "col", None), P(("row", "col"), None, None), P()),
        check_vma=False,
    )
```

```python
import functools

import jax
import jax.numpy as jnp
from jax import lax
from jax.experimental import pallas as pl
from jax.experimental.pallas import tpu as pltpu
from jax.sharding import PartitionSpec as P

EPSILON = 1e-05
MESH = pl.DeviceIdType.MESH
BF = jnp.bfloat16
F32 = jnp.float32


def f32dot(a, b, dims):
    return lax.dot_general(a, b, (dims, ((), ())), preferred_element_type=F32)


def kernel(
    acts_hbm, w1_hbm, w2_hbm, w_hbm, bias_hbm, g_hbm,
    pair_hbm, sens, wg_out,
    acts, bias, scaled_v, inv_v, wcat, wbuf, wf, wc, gcat, lbuf, lm, ltc, xr, rraw, rf, r2d, rt,
    tmat, umat, grb, grx, gf, grs, gry, gry2, grz, gro, gls, glr,
    wg32, wgb, wgx, whb, wy, wzb, wxb, wfin, pbuf,
    s_loc, s_g, s_p, l_s, l_r, a_s, a_r, b_s, b_r, c_s, c_r, x_s, x_r, y_s, y_r, o_s, o_r, gl_s, gl_r,
    w0_s, w0_r, w1_s, w1_r, w2_s, w2_r, w3_s, w3_r, w4_s, w4_r, w5_s, w5_r,
):
    row = lax.axis_index("row")
    col = lax.axis_index("col")
    zl, y, k = row // 16, (row // 2) % 8, row % 2
    zh, x = col // 4, col % 4
    z = zh * 4 + zl
    other = 1 - k
    home = row // 8
    mq = y % 4
    mine = (y + 2) % 4
    y_src = 4 * (col % 2) + mine

    def at(yy, zz, xx=x, kk=k):
        return ((zz % 4) * 16 + yy * 2 + kk, (zz // 4) * 4 + xx)

    y_near = [at((y + d) % 8, z) for d in (1, 7, 2, 6)]
    col_peers = [(row, (col + d) % 8) for d in range(1, 8)]
    x_peers = [at(y, z, (x + d) % 4) for d in range(1, 4)]
    first, second = y * other + z * k, z * other + y * k
    first_peers = [at((y + d * other) % 8, (z + d * k) % 8) for d in range(1, 8)]
    second_peers = [at((y + d * k) % 8, (z + d * other) % 8) for d in range(1, 8)]
    twin = at(y, z, x, other)
    takers = [(a * 16 + ((y + d) % 8) * 2 + k, home) for d in (2, 6) for a in range(4)]
    owners = [(8 * col + 2 * mine + k, c) for c in range(8)]

    def send(src, dst, ss, rs, dev):
        cp = pltpu.make_async_remote_copy(
            src_ref=src, dst_ref=dst, send_sem=ss, recv_sem=rs, device_id=dev, device_id_type=MESH
        )
        cp.start()
        return cp

    def wait_for(dst, ss, rs):
        pltpu.make_async_remote_copy(
            src_ref=dst, dst_ref=dst, send_sem=ss, recv_sem=rs, device_id=twin, device_id_type=MESH
        ).wait_recv()

    loads = [
        pltpu.make_async_copy(src, dst, s_loc.at[n])
        for n, (src, dst) in enumerate(
            [(acts_hbm, acts), (w1_hbm, wcat.at[0:32]), (w2_hbm, wcat.at[32:64]), (w_hbm, wbuf),
             (bias_hbm, bias)]
        )
    ]
    for cp in loads:
        cp.start()

    barrier = pltpu.get_barrier_semaphore()
    greet = takers + owners + col_peers + first_peers + second_peers + y_near + [twin]
    for dev in greet:
        pl.semaphore_signal(barrier, inc=1, device_id=dev, device_id_type=MESH)

    gloads = []
    for i in range(16):
        cp = pltpu.make_async_copy(g_hbm.at[i], gcat.at[:, pl.ds(i * 128, 128)], s_g.at[i])
        cp.start()
        gloads.append(cp)
    wcat[64:128] = jnp.zeros((64, 256), BF)

    loads[0].wait()
    xv = acts[...].astype(F32).reshape(128, 256)
    center = jnp.mean(xv, axis=-1, keepdims=True)
    diff = xv - center
    inv = lax.rsqrt(jnp.mean(diff * diff, axis=-1, keepdims=True) + EPSILON)
    scaled = diff * inv
    scaled_v[...] = scaled
    inv_v[...] = inv
    loads[1].wait()
    loads[2].wait()
    projt = f32dot(wcat[0:64], scaled.astype(BF), ((1,), (1,)))
    low = lax.broadcasted_iota(jnp.int32, (16, 128), 1) < 64
    lbuf[col] = projt[0:32].astype(BF)
    ra, rb = projt[32:48], projt[48:64]
    xr[0:16] = jnp.where(low, ra, pltpu.roll(rb, 64, 1)).astype(BF)
    xr[16:32] = jnp.where(low, pltpu.roll(ra, 64, 1), rb).astype(BF)

    pl.semaphore_wait(barrier, len(greet))

    sent = []
    a_cp = [
        send(xr, rraw.at[mq, k, col], a_s.at[n], a_r.at[col], takers[n]) for n in range(8)
    ]
    l_cp = [
        send(lbuf.at[col], lbuf.at[col], l_s.at[d], l_r.at[d], col_peers[d]) for d in range(7)
    ]
    sent += l_cp + a_cp

    loads[3].wait()
    loads[4].wait()
    wf[...] = wbuf[...].astype(F32)
    for e in range(32):
        pos = (e % 16) * 2 + e // 16
        wc[:, pos * 128:(pos + 1) * 128] = (wf[pl.ds(e, 32, stride=32), :] * (1.0 / 64.0)).astype(BF)

    for cp in l_cp:
        cp.wait_recv()
    for c in range(8):
        blk = lbuf[c]
        ltc[:, c * 128:(c + 1) * 128] = blk
        lm[c * 128:(c + 1) * 128, :] = blk.astype(F32).T.astype(BF)

    for c in range(8):
        wait_for(rraw.at[mine, k, c], a_s.at[c], a_r.at[c])
    part = [(0, 8), (0, 8), (0, 4), (4, 4)]
    b_cp = []
    for n in range(4):
        piece = rraw.at[mine, k, pl.ds(part[n][0], part[n][1])]
        b_cp.append(send(piece, piece, b_s.at[n], b_r.at[n], y_near[n]))
    c_cp = [send(rraw.at[mine, k], rraw.at[mine, k], c_s.at[4], c_r.at[4], twin)]
    sent += b_cp

    def t_step(t, _):
        c0 = pl.multiple_of(t * 256, 256)
        r0 = pl.multiple_of(t * 128, 128)
        for ib in range(2):
            res = f32dot(lm[ib * 512:(ib + 1) * 512, :], wc[:, pl.ds(c0, 256)], ((1,), (0,)))
            res = res.astype(BF)
            for i in range(8):
                for h in range(2):
                    tmat[pl.ds(r0 + h * 64, 64), (ib * 8 + i) * 128:(ib * 8 + i + 1) * 128] = res[
                        i * 64:(i + 1) * 64, h * 128:(h + 1) * 128
                    ]
        return 0

    lax.fori_loop(0, 16, t_step, 0)

    for cp in gloads:
        cp.wait()

    def gr_step(n, _):
        res = f32dot(gcat[...], tmat[pl.ds(pl.multiple_of(n * 256, 256), 256), :], ((1,), (1,)))
        res = res.astype(BF)
        for tt in range(2):
            for q in range(8):
                grb[q % 2, n * 2 + tt, (q // 2) * 16:(q // 2 + 1) * 16, :] = res[
                    q * 16:(q + 1) * 16, tt * 128:(tt + 1) * 128
                ]
        return 0

    lax.fori_loop(0, 4, gr_step, 0)

    for n, off in enumerate((3, 1, 2, 2)):
        piece = rraw.at[(mine + off) % 4, k, pl.ds(part[n][0], part[n][1])]
        wait_for(piece, b_s.at[n], b_r.at[n])
        c_cp.append(send(piece, piece, c_s.at[n], c_r.at[n], twin))
    sent += c_cp
    for cp in c_cp:
        cp.wait_recv()

    def rf_step(n, _):
        blk = rraw[n // 2, n % 2].reshape(256, 128)
        rf[pl.ds(pl.multiple_of(n * 256, 256), 256), :] = blk.astype(F32)
        return 0

    lax.fori_loop(0, 8, rf_step, 0)

    def rt_step(t, _):
        blk = rf[pl.ds(t, 128, stride=16), :]
        t0 = pl.multiple_of(t * 128, 128)
        r2d[:, pl.ds(t0, 128)] = blk.astype(BF)
        rt[pl.ds(t0, 128), :] = blk.T.astype(BF)
        return 0

    lax.fori_loop(0, 16, rt_step, 0)

    def u_step(t, _):
        t0 = pl.multiple_of(t * 128, 128)
        lhs = rt[pl.ds(t0, 128), :]
        for ib in range(2):
            res = f32dot(lhs, gcat[:, ib * 1024:(ib + 1) * 1024], ((1,), (0,))).astype(BF)
            for i in range(8):
                for h in range(2):
                    umat[
                        (ib * 8 + i) * 64:(ib * 8 + i + 1) * 64,
                        pl.ds(pl.multiple_of(t * 256 + h * 128, 128), 128),
                    ] = res[h * 64:(h + 1) * 64, i * 128:(i + 1) * 128]
        return 0

    lax.fori_loop(0, 16, u_step, 0)

    def w_step(n, _):
        wt = f32dot(ltc[...], umat[:, pl.ds(pl.multiple_of(n * 512, 512), 512)], ((1,), (0,)))
        for tt in range(2):
            r0 = pl.multiple_of(n * 64 + tt * 32, 32)
            for h in range(2):
                piece = wt[:, (tt * 2 + h) * 128:(tt * 2 + h + 1) * 128]
                wg32[h, pl.ds(r0, 32), :] = piece
                wgb[h, pl.ds(r0, 32), :] = piece.astype(BF)
        return 0

    lax.fori_loop(0, 8, w_step, 0)

    w0_cp = send(wgb.at[other], wgx, w0_s, w0_r, twin)
    sent.append(w0_cp)
    lax.fori_loop(4, 8, gr_step, 0)
    x_cp = send(grb.at[other], grx, x_s, x_r, twin)
    sent.append(x_cp)
    w0_cp.wait_recv()
    for n in range(8):
        whb[n] = (
            wg32[k, n * 64:(n + 1) * 64, :] + wgx[n * 64:(n + 1) * 64, :].astype(F32)
        ).astype(BF)
    w1_cp = [
        send(whb.at[(first + d + 1) % 8], wy.at[d], w1_s.at[d], w1_r.at[d], first_peers[d])
        for d in range(7)
    ]
    sent += w1_cp

    def gl_step(n, _):
        res = f32dot(wc[...], umat[pl.ds(pl.multiple_of(n * 256, 256), 256), :], ((1,), (1,)))
        res = res.astype(BF)
        gls[n * 2] = res[:, 0:128]
        gls[n * 2 + 1] = res[:, 128:256]
        return 0

    lax.fori_loop(0, 4, gl_step, 0)
    gl_cp = [
        send(gls.at[(col + d + 1) % 8], glr.at[d], gl_s.at[d], gl_r.at[d], col_peers[d])
        for d in range(7)
    ]
    sent += gl_cp

    x_cp.wait_recv()

    def gs_step(t, _):
        gf[pl.ds(t, 64, stride=16), :] = grb[k, t].astype(F32) + grx[t].astype(F32)
        return 0

    lax.fori_loop(0, 16, gs_step, 0)

    def gp_step(m, _):
        blk = gf[pl.ds(pl.multiple_of(m * 256, 256), 256), :].astype(BF)
        grs[m] = blk.reshape(8, 32, 128)
        return 0

    lax.fori_loop(0, 4, gp_step, 0)
    y_cp = []
    for n, off in enumerate((1, 3, 2, 2)):
        piece = grs.at[(mine + off) % 4, pl.ds(part[n][0], part[n][1])]
        dst = gry.at[n] if n < 2 else gry2.at[n - 2]
        y_cp.append(send(piece, dst, y_s.at[n], y_r.at[n], y_near[n]))
    sent += y_cp

    for cp in w1_cp:
        cp.wait_recv()
    acc = whb[first].astype(F32)
    for d in range(7):
        acc = acc + wy[d].astype(F32)
    wzb[second] = acc.astype(BF)
    w2_cp = [
        send(wzb.at[second], wzb.at[second], w2_s.at[d], w2_r.at[d], second_peers[d]) for d in range(7)
    ]
    sent += w2_cp

    def pair_step(n, _):
        c0 = pl.multiple_of(n * 256, 256)
        res = f32dot(r2d[...], tmat[:, pl.ds(c0, 256)], ((1,), (0,)))
        for i in range(2):
            pbuf[n * 2 + i] = (res[:, i * 128:(i + 1) * 128] + bias[...]).astype(BF)
        return 0

    lax.fori_loop(0, 8, pair_step, 0)
    p_cp = pltpu.make_async_copy(pbuf, pair_hbm, s_p)
    p_cp.start()

    for cp in y_cp:
        cp.wait_recv()
    for c in range(8):
        acc = grs[mine, c].astype(F32) + gry[0, c].astype(F32) + gry[1, c].astype(F32)
        grz[c] = (acc + gry2[c // 4, c % 4].astype(F32)).astype(BF)
    slot = zl * 2 + ((y - y_src + 8) % 8) // 4
    o_cp = [send(grz.at[c], gro.at[slot], o_s.at[c], o_r.at[slot], owners[c]) for c in range(8)]
    sent += o_cp

    for cp in w2_cp:
        cp.wait_recv()
    acc = wzb[0].astype(F32)
    for n in range(1, 8):
        acc = acc + wzb[n].astype(F32)
    wxb[x] = acc.astype(BF)
    w3_cp = [
        send(wxb.at[x], wxb.at[x], w3_s.at[d], w3_r.at[d], x_peers[d]) for d in range(3)
    ]
    sent += w3_cp
    for cp in w3_cp:
        cp.wait_recv()
    acc = wxb[0].astype(F32)
    for n in range(1, 4):
        acc = acc + wxb[n].astype(F32)
    wfin[k, first] = acc.astype(BF)
    w4_cp = [
        send(wfin.at[k, first], wfin.at[k, first], w4_s.at[d], w4_r.at[d], first_peers[d])
        for d in range(7)
    ]
    w5_cp = [send(wfin.at[k, first], wfin.at[k, first], w5_s.at[0], w5_r.at[0], twin)]
    sent += w4_cp

    for cp in gl_cp:
        cp.wait_recv()
    gl = gls[col].astype(F32)
    for d in range(7):
        gl = gl + glr[d].astype(F32)
    for n in range(8):
        wait_for(gro.at[n], o_s.at[n], o_r.at[n])
    gr = gro[0].astype(F32)
    for n in range(1, 8):
        gr = gr + gro[n].astype(F32)
    x0, x1 = gr[0:16], gr[16:32]
    ga = jnp.where(low, x0, pltpu.roll(x1, 64, 1))
    gb = jnp.where(low, pltpu.roll(x0, 64, 1), x1)
    gt = jnp.concatenate([gl, ga, gb, jnp.zeros((64, 128), F32)], axis=0).T
    hi = gt.astype(BF)
    rest = gt - hi.astype(F32)
    mid = rest.astype(BF)
    lo = (rest - mid.astype(F32)).astype(BF)
    wv = wcat[...]
    nt = ((1,), (0,))
    gn = f32dot(hi, wv, nt) + (f32dot(mid, wv, nt) + f32dot(lo, wv, nt))
    sc = scaled_v[...]
    mean_grad = jnp.mean(gn, axis=-1, keepdims=True)
    mean_cross = jnp.mean(gn * sc, axis=-1, keepdims=True)
    res = inv_v[...] * (gn - mean_grad - sc * mean_cross)
    sens[...] = res.astype(BF).reshape(2, 64, 256)

    for d in range(7):
        w4_cp[d].wait_recv()
        ys = (first + 7 - d) % 8
        w5_cp.append(
            send(wfin.at[k, ys], wfin.at[k, ys], w5_s.at[d + 1], w5_r.at[d + 1], twin)
        )
    sent += w5_cp
    for cp in w5_cp:
        cp.wait_recv()
    for h in range(2):
        for n in range(8):
            blk = wfin[h, n].astype(F32) * (8.0 / 65536.0)
            for tt in range(2):
                e = h * 16 + n * 2 + tt
                wg_out[pl.ds(e, 32, stride=32), :] = blk[tt * 32:(tt + 1) * 32]
    p_cp.wait()
    for cp in sent:
        cp.wait_send()


def on_device(acts, w1, w2, w, bias, g):
    vm = pl.BlockSpec(memory_space=pltpu.VMEM)
    anys = pl.BlockSpec(memory_space=pl.ANY)
    dma = pltpu.SemaphoreType.DMA
    scratch = [
        ((2, 64, 256), BF), ((1, 128), F32),
        ((128, 256), F32), ((128, 1), F32), ((128, 256), BF), ((1024, 128), BF), ((1024, 128), F32),
        ((32, 4096), BF), ((128, 2048), BF), ((8, 32, 128), BF), ((1024, 32), BF), ((32, 1024), BF),
        ((32, 128), BF), ((4, 2, 8, 32, 128), BF), ((2048, 128), F32), ((128, 2048), BF),
        ((2048, 128), BF),
        ((2048, 2048), BF), ((1024, 4096), BF), ((2, 16, 64, 128), BF), ((16, 64, 128), BF),
        ((1024, 128), F32), ((4, 8, 32, 128), BF), ((2, 8, 32, 128), BF), ((2, 4, 32, 128), BF),
        ((8, 32, 128), BF), ((8, 32, 128), BF), ((8, 32, 128), BF), ((7, 32, 128), BF),
        ((2, 512, 128), F32), ((2, 512, 128), BF), ((512, 128), BF), ((8, 64, 128), BF),
        ((7, 64, 128), BF), ((8, 64, 128), BF), ((4, 64, 128), BF), ((2, 8, 64, 128), BF),
        ((16, 128, 128), BF),
    ]
    scratch = [pltpu.VMEM(s, d) for s, d in scratch]
    scratch += [dma((5,)), dma((16,)), dma]
    for n in (7, 8, 4, 5, 0, 4, 8, 7, 0, 7, 7, 3, 7, 8):
        scratch += [dma((n,)), dma((n,))] if n else [dma, dma]
    return pl.pallas_call(
        kernel,
        out_shape=(
            jax.ShapeDtypeStruct((16, 128, 128), BF),
            jax.ShapeDtypeStruct((2, 64, 256), BF),
            jax.ShapeDtypeStruct((1024, 128), F32),
        ),
        in_specs=[anys] * 6,
        out_specs=(anys, vm, vm),
        scratch_shapes=scratch,
        compiler_params=pltpu.CompilerParams(
            collective_id=0, has_side_effects=True, vmem_limit_bytes=64 * 2**20 - 65536
        ),
    )(acts, w1.T, w2.T, w, bias.reshape(1, 128), g)


def solution(mesh):
    return jax.shard_map(
        on_device,
        mesh=mesh,
        in_specs=(P(("row", "col"), None, None), P(), P(), P(), P(), P("row", "col", None)),
        out_specs=(P("row", "col", None), P(("row", "col"), None, None), P()),
        check_vma=False,
    )
```

```python
import functools

import jax
import jax.numpy as jnp
from jax import lax
from jax.experimental import pallas as pl
from jax.experimental.pallas import tpu as pltpu
from jax.sharding import PartitionSpec as P

EPSILON = 1e-05
MESH = pl.DeviceIdType.MESH
BF = jnp.bfloat16
FAR = (4, 3, 5, 2, 6, 1, 7)
F32 = jnp.float32


def f32dot(a, b, dims):
    return lax.dot_general(a, b, (dims, ((), ())), preferred_element_type=F32)


def kernel(
    acts_hbm, w1_hbm, w2_hbm, w_hbm, bias_hbm, g_hbm,
    pair_hbm, sens_hbm, wg_hbm,
    acts, bias, scaled_v, inv_v, wcat, wbuf, wf, wc, gcat, lbuf, lm, ltc, xr, rraw, rf, r2d, rt,
    tmat, umat, grb, grx, gf, grs, gry, gry2, grz, gro, gls, glr,
    wg32, wgb, wgx, whb, wy, wzb, wxb, wfin, pbuf, sens, wg_out,
    s_loc, s_g, s_out, l_s, l_r, a_s, a_r, b_s, b_r, c_s, c_r, x_s, x_r, y_s, y_r, o_s, o_r, gl_s, gl_r,
    w0_s, w0_r, w1_s, w1_r, w2_s, w2_r, w3_s, w3_r, w4_s, w4_r, w5_s, w5_r,
):
    row = lax.axis_index("row")
    col = lax.axis_index("col")
    zl, y, k = row // 16, (row // 2) % 8, row % 2
    zh, x = col // 4, col % 4
    z = zh * 4 + zl
    other = 1 - k
    home = row // 8
    mq = y % 4
    mine = (y + 2) % 4
    y_src = 4 * (col % 2) + mine

    def at(yy, zz, xx=x, kk=k):
        return ((zz % 4) * 16 + yy * 2 + kk, (zz // 4) * 4 + xx)

    y_near = [at((y + d) % 8, z) for d in (2, 6, 1, 7)]
    col_peers = [(row, (col + d) % 8) for d in FAR]
    x_peers = [at(y, z, (x + d) % 4) for d in range(1, 4)]
    first, second = y * other + z * k, z * other + y * k
    first_peers = [at((y + d * other) % 8, (z + d * k) % 8) for d in FAR]
    second_peers = [at((y + d * k) % 8, (z + d * other) % 8) for d in FAR]
    twin = at(y, z, x, other)
    takers = [(a * 16 + ((y + d) % 8) * 2 + k, home) for d in (2, 6) for a in range(4)]
    owners = [(8 * col + 2 * mine + k, c) for c in range(8)]

    def send(src, dst, ss, rs, dev):
        cp = pltpu.make_async_remote_copy(
            src_ref=src, dst_ref=dst, send_sem=ss, recv_sem=rs, device_id=dev, device_id_type=MESH
        )
        cp.start()
        return cp

    def wait_for(dst, ss, rs):
        pltpu.make_async_remote_copy(
            src_ref=dst, dst_ref=dst, send_sem=ss, recv_sem=rs, device_id=twin, device_id_type=MESH
        ).wait_recv()

    loads = [
        pltpu.make_async_copy(src, dst, s_loc.at[n])
        for n, (src, dst) in enumerate(
            [(acts_hbm, acts), (w1_hbm, wcat.at[0:32]), (w2_hbm, wcat.at[32:64]), (w_hbm, wbuf),
             (bias_hbm, bias)]
        )
    ]
    for cp in loads:
        cp.start()

    barrier = pltpu.get_barrier_semaphore()
    greet = takers + owners + col_peers + [at((y + d) % 8, z) for d in FAR]
    greet += [at(y, (z + d) % 8) for d in FAR[1:]] + [twin]
    for dev in greet:
        pl.semaphore_signal(barrier, inc=1, device_id=dev, device_id_type=MESH)

    wcat[64:128] = jnp.zeros((64, 256), BF)

    loads[0].wait()
    xv = acts[...].astype(F32).reshape(128, 256)
    center = jnp.mean(xv, axis=-1, keepdims=True)
    diff = xv - center
    inv = lax.rsqrt(jnp.mean(diff * diff, axis=-1, keepdims=True) + EPSILON)
    scaled = diff * inv
    scaled_v[...] = scaled
    inv_v[...] = inv
    loads[1].wait()
    loads[2].wait()
    projt = f32dot(wcat[0:64], scaled.astype(BF), ((1,), (1,)))
    low = lax.broadcasted_iota(jnp.int32, (16, 128), 1) < 64
    lbuf[col] = projt[0:32].astype(BF)
    ra, rb = projt[32:48], projt[48:64]
    xr[0:16] = jnp.where(low, ra, pltpu.roll(rb, 64, 1)).astype(BF)
    xr[16:32] = jnp.where(low, pltpu.roll(ra, 64, 1), rb).astype(BF)

    pl.semaphore_wait(barrier, len(greet))

    a_cp = [
        send(xr, rraw.at[mq, k, col], a_s.at[n], a_r.at[col], takers[n]) for n in range(8)
    ]
    l_cp = [
        send(lbuf.at[col], lbuf.at[col], l_s.at[d], l_r.at[d], col_peers[d]) for d in range(7)
    ]

    gloads = []
    for i in range(16):
        cp = pltpu.make_async_copy(g_hbm.at[i], gcat.at[:, pl.ds(i * 128, 128)], s_g.at[i])
        cp.start()
        gloads.append(cp)

    loads[3].wait()
    loads[4].wait()
    wf[...] = wbuf[...].astype(F32)
    for e in range(32):
        pos = (e % 16) * 2 + e // 16
        wc[:, pos * 128:(pos + 1) * 128] = (wf[pl.ds(e, 32, stride=32), :] * (1.0 / 64.0)).astype(BF)

    for cp in l_cp:
        cp.wait_recv()
    for c in range(8):
        blk = lbuf[c]
        ltc[:, c * 128:(c + 1) * 128] = blk
        lm[c * 128:(c + 1) * 128, :] = blk.astype(F32).T.astype(BF)

    for c in range(8):
        wait_for(rraw.at[mine, k, c], a_s.at[c], a_r.at[c])
    part = [(0, 4), (4, 4), (0, 8), (0, 8)]
    b_cp = []
    for n in range(4):
        piece = rraw.at[mine, k, pl.ds(part[n][0], part[n][1])]
        b_cp.append(send(piece, piece, b_s.at[n], b_r.at[n], y_near[n]))
    c_cp = [send(rraw.at[mine, k], rraw.at[mine, k], c_s.at[4], c_r.at[4], twin)]

    def t_step(n, _):
        for ib in range(8):
            for tt in range(4):
                c0 = pl.multiple_of(n * 1024 + tt * 256, 256)
                r0 = pl.multiple_of(n * 512 + tt * 128, 128)
                res = f32dot(lm[ib * 128:(ib + 1) * 128, :], wc[:, pl.ds(c0, 256)], ((1,), (0,)))
                res = res.astype(BF)
                for i in range(2):
                    for h in range(2):
                        tmat[
                            pl.ds(r0 + h * 64, 64), (ib * 2 + i) * 128:(ib * 2 + i + 1) * 128
                        ] = res[i * 64:(i + 1) * 64, h * 128:(h + 1) * 128]
        return 0

    lax.fori_loop(0, 4, t_step, 0)

    for cp in gloads:
        cp.wait()

    def gr_step(n, _):
        res = f32dot(gcat[...], tmat[pl.ds(pl.multiple_of(n * 512, 512), 512), :], ((1,), (1,)))
        res = res.astype(BF)
        for tt in range(4):
            for q in range(8):
                grb[q % 2, n * 4 + tt, (q // 2) * 16:(q // 2 + 1) * 16, :] = res[
                    q * 16:(q + 1) * 16, tt * 128:(tt + 1) * 128
                ]
        return 0

    lax.fori_loop(0, 2, gr_step, 0)

    for n, off in ((2, 3), (3, 1), (0, 2), (1, 2)):
        piece = rraw.at[(mine + off) % 4, k, pl.ds(part[n][0], part[n][1])]
        wait_for(piece, b_s.at[n], b_r.at[n])
        c_cp.append(send(piece, piece, c_s.at[n], c_r.at[n], twin))

    def spread(kk):
        for m in range(4):
            r0 = pl.multiple_of((m * 2 + kk) * 256, 256)
            rf[pl.ds(r0, 256), :] = rraw[m, kk].reshape(256, 128).astype(F32)

    spread(k)
    for cp in c_cp:
        cp.wait_recv()
    spread(other)
    for t in range(16):
        blk = rf[pl.ds(t, 128, stride=16), :].astype(BF)
        r2d[:, t * 128:(t + 1) * 128] = blk
        rt[t * 128:(t + 1) * 128, :] = blk.T

    def u_step(n, _):
        rhs = gcat[:, pl.ds(pl.multiple_of(n * 256, 256), 256)]
        for t in range(16):
            res = f32dot(rt[t * 128:(t + 1) * 128, :], rhs, ((1,), (0,))).astype(BF)
            for i in range(2):
                for h in range(2):
                    umat[
                        pl.ds(pl.multiple_of((n * 2 + i) * 64, 64), 64),
                        t * 256 + h * 128:t * 256 + (h + 1) * 128,
                    ] = res[h * 64:(h + 1) * 64, i * 128:(i + 1) * 128]
        return 0

    lax.fori_loop(0, 8, u_step, 0)

    def w_step(n, _):
        wt = f32dot(ltc[...], umat[:, pl.ds(pl.multiple_of(n * 1024, 1024), 1024)], ((1,), (0,)))
        for tt in range(4):
            r0 = pl.multiple_of(n * 128 + tt * 32, 32)
            for h in range(2):
                piece = wt[:, (tt * 2 + h) * 128:(tt * 2 + h + 1) * 128]
                wg32[h, pl.ds(r0, 32), :] = piece
                wgb[h, pl.ds(r0, 32), :] = piece.astype(BF)
        return 0

    lax.fori_loop(0, 4, w_step, 0)

    w0_cp = send(wgb.at[other], wgx, w0_s, w0_r, twin)
    w0_cp.wait_recv()
    for n in range(8):
        whb[n] = (
            wg32[k, n * 64:(n + 1) * 64, :] + wgx[n * 64:(n + 1) * 64, :].astype(F32)
        ).astype(BF)
    w1_cp = [
        send(whb.at[(first + FAR[d]) % 8], wy.at[d], w1_s.at[d], w1_r.at[d], first_peers[d])
        for d in range(7)
    ]
    lax.fori_loop(2, 4, gr_step, 0)
    x_cp = send(grb.at[other], grx, x_s, x_r, twin)

    def gl_step(n, _):
        res = f32dot(wc[...], umat[pl.ds(pl.multiple_of(n * 512, 512), 512), :], ((1,), (1,)))
        res = res.astype(BF)
        for c in range(4):
            gls[n * 4 + c] = res[:, c * 128:(c + 1) * 128]
        return 0

    lax.fori_loop(0, 2, gl_step, 0)
    gl_cp = [
        send(gls.at[(col + FAR[d]) % 8], glr.at[d], gl_s.at[d], gl_r.at[d], col_peers[d])
        for d in range(7)
    ]

    x_cp.wait_recv()

    def gs_step(t, _):
        gf[pl.ds(t, 64, stride=16), :] = grb[k, t].astype(F32) + grx[t].astype(F32)
        return 0

    lax.fori_loop(0, 16, gs_step, 0)

    def gp_step(m, _):
        blk = gf[pl.ds(pl.multiple_of(m * 256, 256), 256), :].astype(BF)
        grs[m] = blk.reshape(8, 32, 128)
        return 0

    lax.fori_loop(0, 4, gp_step, 0)
    y_cp = []
    for n, off in enumerate((2, 2, 1, 3)):
        piece = grs.at[(mine + off) % 4, pl.ds(part[n][0], part[n][1])]
        dst = gry2.at[n] if n < 2 else gry.at[n - 2]
        y_cp.append(send(piece, dst, y_s.at[n], y_r.at[n], y_near[n]))

    for cp in l_cp + a_cp + b_cp + c_cp + [w0_cp, x_cp]:
        cp.wait_send()
    for cp in w1_cp:
        cp.wait_recv()
    acc = whb[first].astype(F32)
    for d in range(7):
        acc = acc + wy[d].astype(F32)
    wzb[second] = acc.astype(BF)
    w2_cp = [
        send(wzb.at[second], wzb.at[second], w2_s.at[d], w2_r.at[d], second_peers[d]) for d in range(7)
    ]

    def pair_step(n, _):
        c0 = pl.multiple_of(n * 512, 512)
        res = f32dot(r2d[...], tmat[:, pl.ds(c0, 512)], ((1,), (0,)))
        for i in range(4):
            pbuf[n * 4 + i] = (res[:, i * 128:(i + 1) * 128] + bias[...]).astype(BF)
        return 0

    lax.fori_loop(0, 4, pair_step, 0)
    p_cp = pltpu.make_async_copy(pbuf, pair_hbm, s_out.at[0])
    p_cp.start()

    for cp in y_cp:
        cp.wait_recv()
    for c in range(8):
        acc = grs[mine, c].astype(F32) + gry[0, c].astype(F32) + gry[1, c].astype(F32)
        grz[c] = (acc + gry2[c // 4, c % 4].astype(F32)).astype(BF)
    slot = zl * 2 + ((y - y_src + 8) % 8) // 4
    o_cp = [send(grz.at[c], gro.at[slot], o_s.at[c], o_r.at[slot], owners[c]) for c in range(8)]

    for cp in w1_cp + gl_cp + y_cp:
        cp.wait_send()
    for cp in w2_cp:
        cp.wait_recv()
    acc = wzb[0].astype(F32)
    for n in range(1, 8):
        acc = acc + wzb[n].astype(F32)
    wxb[x] = acc.astype(BF)
    w3_cp = [
        send(wxb.at[x], wxb.at[x], w3_s.at[d], w3_r.at[d], x_peers[d]) for d in range(3)
    ]
    for cp in w3_cp:
        cp.wait_recv()
    acc = wxb[0].astype(F32)
    for n in range(1, 4):
        acc = acc + wxb[n].astype(F32)
    wfin[k, first] = acc.astype(BF)
    w4_cp = [
        send(wfin.at[k, first], wfin.at[k, first], w4_s.at[d], w4_r.at[d], first_peers[d])
        for d in range(7)
    ]
    w5_cp = [send(wfin.at[k, first], wfin.at[k, first], w5_s.at[0], w5_r.at[0], twin)]

    for cp in gl_cp:
        cp.wait_recv()
    gl = gls[col].astype(F32)
    for d in range(7):
        gl = gl + glr[d].astype(F32)
    for n in range(8):
        wait_for(gro.at[n], o_s.at[n], o_r.at[n])
    gr = gro[0].astype(F32)
    for n in range(1, 8):
        gr = gr + gro[n].astype(F32)
    x0, x1 = gr[0:16], gr[16:32]
    ga = jnp.where(low, x0, pltpu.roll(x1, 64, 1))
    gb = jnp.where(low, pltpu.roll(x0, 64, 1), x1)
    gt = jnp.concatenate([gl, ga, gb, jnp.zeros((64, 128), F32)], axis=0).T
    hi = gt.astype(BF)
    rest = gt - hi.astype(F32)
    mid = rest.astype(BF)
    lo = (rest - mid.astype(F32)).astype(BF)
    wv = wcat[...]
    nt = ((1,), (0,))
    gn = f32dot(hi, wv, nt) + (f32dot(mid, wv, nt) + f32dot(lo, wv, nt))
    sc = scaled_v[...]
    mean_grad = jnp.mean(gn, axis=-1, keepdims=True)
    mean_cross = jnp.mean(gn * sc, axis=-1, keepdims=True)
    res = inv_v[...] * (gn - mean_grad - sc * mean_cross)
    sens[...] = res.astype(BF).reshape(2, 64, 256)
    s_cp = pltpu.make_async_copy(sens, sens_hbm, s_out.at[1])
    s_cp.start()
    for cp in o_cp + w2_cp + w3_cp:
        cp.wait_send()
    p_cp.wait()

    for d in range(6, -1, -1):
        w4_cp[d].wait_recv()
        ys = (first + 8 - FAR[d]) % 8
        w5_cp.append(
            send(wfin.at[k, ys], wfin.at[k, ys], w5_s.at[d + 1], w5_r.at[d + 1], twin)
        )
    for cp in w5_cp:
        cp.wait_recv()
    for h in range(2):
        for n in range(8):
            blk = wfin[h, n].astype(F32) * (8.0 / 65536.0)
            for tt in range(2):
                e = h * 16 + n * 2 + tt
                wg_out[pl.ds(e, 32, stride=32), :] = blk[tt * 32:(tt + 1) * 32]
    wg_cp = pltpu.make_async_copy(wg_out, wg_hbm, s_out.at[2])
    wg_cp.start()
    s_cp.wait()
    for cp in w4_cp + w5_cp:
        cp.wait_send()
    wg_cp.wait()


def hand_over(pair, sens, wg, pair_out, sens_out, wg_out, pair_v, sens_v, wg_v, sem_in, sem_out):
    trips = [(sens, sens_v, sens_out)]
    for n in range(2):
        part = pl.ds(n * 512, 512)
        trips.append((wg.at[part], wg_v.at[part], wg_out.at[part]))
    for n in range(2):
        part = pl.ds(n * 8, 8)
        trips.append((pair.at[part], pair_v.at[part], pair_out.at[part]))
    ins = [pltpu.make_async_copy(a, b, sem_in.at[n]) for n, (a, b, _) in enumerate(trips)]
    outs = [pltpu.make_async_copy(b, c, sem_out.at[n]) for n, (_, b, c) in enumerate(trips)]
    for cp in ins:
        cp.start()
    for a, b in zip(ins, outs):
        a.wait()
        b.start()
    for cp in outs:
        cp.wait()


def on_device(acts, w1, w2, w, bias, g):
    anys = pl.BlockSpec(memory_space=pl.ANY)
    dma = pltpu.SemaphoreType.DMA
    scratch = [
        ((2, 64, 256), BF), ((1, 128), F32),
        ((128, 256), F32), ((128, 1), F32), ((128, 256), BF), ((1024, 128), BF), ((1024, 128), F32),
        ((32, 4096), BF), ((128, 2048), BF), ((8, 32, 128), BF), ((1024, 32), BF), ((32, 1024), BF),
        ((32, 128), BF), ((4, 2, 8, 32, 128), BF), ((2048, 128), F32), ((128, 2048), BF),
        ((2048, 128), BF),
        ((2048, 2048), BF), ((1024, 4096), BF), ((2, 16, 64, 128), BF), ((16, 64, 128), BF),
        ((1024, 128), F32), ((4, 8, 32, 128), BF), ((2, 8, 32, 128), BF), ((2, 4, 32, 128), BF),
        ((8, 32, 128), BF), ((8, 32, 128), BF), ((8, 32, 128), BF), ((7, 32, 128), BF),
        ((2, 512, 128), F32), ((2, 512, 128), BF), ((512, 128), BF), ((8, 64, 128), BF),
        ((7, 64, 128), BF), ((8, 64, 128), BF), ((4, 64, 128), BF), ((2, 8, 64, 128), BF),
        ((16, 128, 128), BF), ((2, 64, 256), BF), ((1024, 128), F32),
    ]
    scratch = [pltpu.VMEM(s, d) for s, d in scratch]
    scratch += [dma((5,)), dma((16,)), dma((3,))]
    for n in (7, 8, 4, 5, 0, 4, 8, 7, 0, 7, 7, 3, 7, 8):
        scratch += [dma((n,)), dma((n,))] if n else [dma, dma]
    shapes = (
        jax.ShapeDtypeStruct((16, 128, 128), BF),
        jax.ShapeDtypeStruct((2, 64, 256), BF),
        jax.ShapeDtypeStruct((1024, 128), F32),
    )
    results = pl.pallas_call(
        kernel,
        out_shape=shapes,
        in_specs=[anys] * 6,
        out_specs=(anys,) * 3,
        scratch_shapes=scratch,
        compiler_params=pltpu.CompilerParams(
            collective_id=0, has_side_effects=True, vmem_limit_bytes=64 * 2**20 - 65536
        ),
    )(acts, w1.T, w2.T, w, bias.reshape(1, 128), g)
    return pl.pallas_call(
        hand_over,
        out_shape=shapes,
        in_specs=[anys] * 3,
        out_specs=(anys,) * 3,
        scratch_shapes=[pltpu.VMEM(o.shape, o.dtype) for o in shapes] + [dma((5,)), dma((5,))],
    )(*results)


def solution(mesh):
    return jax.shard_map(
        on_device,
        mesh=mesh,
        in_specs=(P(("row", "col"), None, None), P(), P(), P(), P(), P("row", "col", None)),
        out_specs=(P("row", "col", None), P(("row", "col"), None, None), P()),
        check_vma=False,
    )
```

```python
import functools

import jax
import jax.numpy as jnp
from jax import lax
from jax.experimental import pallas as pl
from jax.experimental.pallas import tpu as pltpu
from jax.sharding import PartitionSpec as P

EPSILON = 1e-05
MESH = pl.DeviceIdType.MESH
BF = jnp.bfloat16
F32 = jnp.float32


def f32dot(a, b, dims):
    return lax.dot_general(a, b, (dims, ((), ())), preferred_element_type=F32)


class Batch:
    def __init__(self, count, make, start=True):
        self.count, self.make = count, make
        if start:
            self.each(lambda cp: cp.start())

    def each(self, act):
        def body(n, _):
            act(self.make(n))
            return 0

        lax.fori_loop(0, self.count, body, 0)

    def wait_recv(self):
        self.each(lambda cp: cp.wait_recv())

    def wait_send(self):
        self.each(lambda cp: cp.wait_send())


def kernel(
    acts_hbm, w1_hbm, w2_hbm, w_hbm, bias_hbm, g_hbm,
    pair_hbm, sens_hbm, wfin_hbm,
    acts, bias, scaled_v, inv_v, wcat, wbuf, wf, wc, gcat, lbuf, lm, ltc, xr, rraw, rf, r2d, rt,
    tmat, umat, grb, grx, gf, grs, gry, gry2, grz, gro, gls, glr,
    wg32, wgb, wgx, whb, wy, wzb, wxb, wfin, pbuf, sens,
    s_loc, s_g, s_out, l_s, l_r, a_s, a_r, b_s, b_r, c_s, c_r, x_s, x_r, y_s, y_r, o_s, o_r, gl_s, gl_r,
    w0_s, w0_r, w1_s, w1_r, w2_s, w2_r, w3_s, w3_r, w4_s, w4_r, w5_s, w5_r,
):
    row = lax.axis_index("row")
    col = lax.axis_index("col")
    zl, y, k = row // 16, (row // 2) % 8, row % 2
    zh, x = col // 4, col % 4
    z = zh * 4 + zl
    other = 1 - k
    home = row // 8
    mq = y % 4
    mine = (y + 2) % 4
    y_src = 4 * (col % 2) + mine

    def at(yy, zz, xx=x, kk=k):
        return ((zz % 4) * 16 + yy * 2 + kk, (zz // 4) * 4 + xx)

    y_near = [at((y + d) % 8, z) for d in (2, 6, 1, 7)]
    x_peers = [at(y, z, (x + d) % 4) for d in range(1, 4)]
    first, second = y * other + z * k, z * other + y * k
    twin = at(y, z, x, other)

    def link(src, dst, ss, rs, dev):
        return pltpu.make_async_remote_copy(
            src_ref=src, dst_ref=dst, send_sem=ss, recv_sem=rs, device_id=dev, device_id_type=MESH
        )

    def send(src, dst, ss, rs, dev):
        cp = link(src, dst, ss, rs, dev)
        cp.start()
        return cp

    def far(n):
        return 4 + (1 - n % 2) * (n // 2) - (n % 2) * ((n + 1) // 2)

    def first_peer(n):
        return at((y + far(n) * other) % 8, (z + far(n) * k) % 8)

    def second_peer(n):
        return at((y + far(n) * k) % 8, (z + far(n) * other) % 8)

    def wait_for(dst, ss, rs):
        pltpu.make_async_remote_copy(
            src_ref=dst, dst_ref=dst, send_sem=ss, recv_sem=rs, device_id=twin, device_id_type=MESH
        ).wait_recv()

    barrier = pltpu.get_barrier_semaphore()

    def greet(dev):
        pl.semaphore_signal(barrier, inc=1, device_id=dev, device_id_type=MESH)

    def greet_far(n, _):
        greet(((n % 4) * 16 + ((y + 2 + 4 * (n // 4)) % 8) * 2 + k, home))
        greet((8 * col + 2 * mine + k, n))
        return 0

    def greet_ring(d, _):
        greet(at((y + d) % 8, z))
        greet(at(y, (z + d) % 8))
        greet((row, (col + d) % 8))
        return 0

    lax.fori_loop(0, 8, greet_far, 0)
    lax.fori_loop(1, 8, greet_ring, 0)
    greet(twin)

    loads = [
        pltpu.make_async_copy(src, dst, s_loc.at[n])
        for n, (src, dst) in enumerate(
            [(acts_hbm, acts), (w1_hbm, wcat.at[0:32]), (w2_hbm, wcat.at[32:64]), (w_hbm, wbuf),
             (bias_hbm, bias)]
        )
    ]
    for cp in loads:
        cp.start()

    wcat[64:128] = jnp.zeros((64, 256), BF)

    loads[0].wait()
    xv = acts[...].astype(F32).reshape(128, 256)
    center = jnp.mean(xv, axis=-1, keepdims=True)
    diff = xv - center
    inv = lax.rsqrt(jnp.mean(diff * diff, axis=-1, keepdims=True) + EPSILON)
    scaled = diff * inv
    scaled_v[...] = scaled
    inv_v[...] = inv
    loads[1].wait()
    loads[2].wait()
    projt = f32dot(wcat[0:64], scaled.astype(BF), ((1,), (1,)))
    low = lax.broadcasted_iota(jnp.int32, (16, 128), 1) < 64
    lbuf[col] = projt[0:32].astype(BF)
    ra, rb = projt[32:48], projt[48:64]
    xr[0:16] = jnp.where(low, ra, pltpu.roll(rb, 64, 1)).astype(BF)
    xr[16:32] = jnp.where(low, pltpu.roll(ra, 64, 1), rb).astype(BF)

    pl.semaphore_wait(barrier, 38)

    def a_copy(n):
        dev = ((n % 4) * 16 + ((y + 2 + 4 * (n // 4)) % 8) * 2 + k, home)
        return link(xr, rraw.at[mq, k, col], a_s.at[n], a_r.at[col], dev)

    def l_copy(n):
        return link(lbuf.at[col], lbuf.at[col], l_s.at[n], l_r.at[n], (row, (col + far(n)) % 8))

    a_cp = [Batch(8, a_copy)]
    l_cp = [Batch(7, l_copy)]

    gloads = []
    for i in range(16):
        cp = pltpu.make_async_copy(g_hbm.at[i], gcat.at[:, pl.ds(i * 128, 128)], s_g.at[i])
        cp.start()
        gloads.append(cp)

    loads[3].wait()
    loads[4].wait()
    wf[...] = wbuf[...].astype(F32)
    for e in range(32):
        pos = (e % 16) * 2 + e // 16
        wc[:, pos * 128:(pos + 1) * 128] = (wf[pl.ds(e, 32, stride=32), :] * (1.0 / 64.0)).astype(BF)

    for c in range(8):
        wait_for(rraw.at[mine, k, c], a_s.at[c], a_r.at[c])
    part = [(0, 4), (4, 4), (0, 8), (0, 8)]
    b_cp = []
    for n in range(4):
        piece = rraw.at[mine, k, pl.ds(part[n][0], part[n][1])]
        b_cp.append(send(piece, piece, b_s.at[n], b_r.at[n], y_near[n]))
    c_cp = [send(rraw.at[mine, k], rraw.at[mine, k], c_s.at[4], c_r.at[4], twin)]

    for cp in l_cp:
        cp.wait_recv()
    for c in range(8):
        blk = lbuf[c]
        ltc[:, c * 128:(c + 1) * 128] = blk
        lm[c * 128:(c + 1) * 128, :] = blk.astype(F32).T.astype(BF)

    def t_step(n, _):
        for ib in range(8):
            for tt in range(4):
                c0 = pl.multiple_of(n * 1024 + tt * 256, 256)
                r0 = pl.multiple_of(n * 512 + tt * 128, 128)
                res = f32dot(lm[ib * 128:(ib + 1) * 128, :], wc[:, pl.ds(c0, 256)], ((1,), (0,)))
                res = res.astype(BF)
                for i in range(2):
                    for h in range(2):
                        tmat[
                            pl.ds(r0 + h * 64, 64), (ib * 2 + i) * 128:(ib * 2 + i + 1) * 128
                        ] = res[i * 64:(i + 1) * 64, h * 128:(h + 1) * 128]
        return 0

    lax.fori_loop(0, 4, t_step, 0)

    for cp in gloads:
        cp.wait()

    def gr_step(n, _):
        res = f32dot(gcat[...], tmat[pl.ds(pl.multiple_of(n * 512, 512), 512), :], ((1,), (1,)))
        res = res.astype(BF)
        for tt in range(4):
            for q in range(8):
                grb[q % 2, n * 4 + tt, (q // 2) * 16:(q // 2 + 1) * 16, :] = res[
                    q * 16:(q + 1) * 16, tt * 128:(tt + 1) * 128
                ]
        return 0

    lax.fori_loop(0, 2, gr_step, 0)

    for n, off in ((2, 3), (3, 1), (0, 2), (1, 2)):
        piece = rraw.at[(mine + off) % 4, k, pl.ds(part[n][0], part[n][1])]
        wait_for(piece, b_s.at[n], b_r.at[n])
        c_cp.append(send(piece, piece, c_s.at[n], c_r.at[n], twin))

    def spread(kk):
        for m in range(4):
            r0 = pl.multiple_of((m * 2 + kk) * 256, 256)
            rf[pl.ds(r0, 256), :] = rraw[m, kk].reshape(256, 128).astype(F32)

    spread(k)
    for cp in c_cp:
        cp.wait_recv()
    spread(other)
    for t in range(16):
        blk = rf[pl.ds(t, 128, stride=16), :].astype(BF)
        r2d[:, t * 128:(t + 1) * 128] = blk
        rt[t * 128:(t + 1) * 128, :] = blk.T

    def u_step(n, _):
        rhs = gcat[:, pl.ds(pl.multiple_of(n * 256, 256), 256)]
        for t in range(16):
            res = f32dot(rt[t * 128:(t + 1) * 128, :], rhs, ((1,), (0,))).astype(BF)
            for i in range(2):
                for h in range(2):
                    umat[
                        pl.ds(pl.multiple_of((n * 2 + i) * 64, 64), 64),
                        t * 256 + h * 128:t * 256 + (h + 1) * 128,
                    ] = res[h * 64:(h + 1) * 64, i * 128:(i + 1) * 128]
        return 0

    lax.fori_loop(0, 8, u_step, 0)

    w0_cp = []
    for n in range(4):
        wt = f32dot(ltc[...], umat[:, n * 1024:(n + 1) * 1024], ((1,), (0,)))
        for tt in range(4):
            r0 = n * 128 + tt * 32
            for h in range(2):
                piece = wt[:, (tt * 2 + h) * 128:(tt * 2 + h + 1) * 128]
                wg32[h, r0:r0 + 32, :] = piece
                wgb[h, r0:r0 + 32, :] = piece.astype(BF)
        rows = pl.ds(n * 128, 128)
        w0_cp.append(send(wgb.at[other, rows], wgx.at[rows], w0_s.at[n], w0_r.at[n], twin))
    for n in range(4):
        w0_cp[n].wait_recv()
        for b in range(2 * n, 2 * n + 2):
            whb[b] = (
                wg32[k, b * 64:(b + 1) * 64, :] + wgx[b * 64:(b + 1) * 64, :].astype(F32)
            ).astype(BF)
    def w1_copy(n):
        return link(
            whb.at[(first + far(n)) % 8], wy.at[n], w1_s.at[n], w1_r.at[n], first_peer(n)
        )

    w1_cp = [Batch(7, w1_copy)]

    lax.fori_loop(2, 4, gr_step, 0)
    x_cp = send(grb.at[other], grx, x_s, x_r, twin)

    def pair_step(n, _):
        c0 = pl.multiple_of(n * 512, 512)
        res = f32dot(r2d[...], tmat[:, pl.ds(c0, 512)], ((1,), (0,)))
        for i in range(4):
            pbuf[n * 4 + i] = (res[:, i * 128:(i + 1) * 128] + bias[...]).astype(BF)
        return 0

    lax.fori_loop(0, 4, pair_step, 0)
    p_cp = pltpu.make_async_copy(pbuf, pair_hbm, s_out.at[0])
    p_cp.start()

    x_cp.wait_recv()

    def gs_step(t, _):
        gf[pl.ds(t, 64, stride=16), :] = grb[k, t].astype(F32) + grx[t].astype(F32)
        return 0

    lax.fori_loop(0, 16, gs_step, 0)

    def gp_step(m, _):
        blk = gf[pl.ds(pl.multiple_of(m * 256, 256), 256), :].astype(BF)
        grs[m] = blk.reshape(8, 32, 128)
        return 0

    lax.fori_loop(0, 4, gp_step, 0)
    y_cp = []
    for n, off in enumerate((2, 2, 1, 3)):
        piece = grs.at[(mine + off) % 4, pl.ds(part[n][0], part[n][1])]
        dst = gry2.at[n] if n < 2 else gry.at[n - 2]
        y_cp.append(send(piece, dst, y_s.at[n], y_r.at[n], y_near[n]))

    for cp in l_cp + a_cp + b_cp + c_cp + w0_cp + [x_cp]:
        cp.wait_send()
    for cp in w1_cp:
        cp.wait_recv()
    acc = whb[first].astype(F32)
    for d in range(7):
        acc = acc + wy[d].astype(F32)
    wzb[second] = acc.astype(BF)

    def w2_copy(n):
        return link(wzb.at[second], wzb.at[second], w2_s.at[n], w2_r.at[n], second_peer(n))

    w2_cp = [Batch(7, w2_copy)]

    def gl_step(n, _):
        res = f32dot(wc[...], umat[pl.ds(pl.multiple_of(n * 512, 512), 512), :], ((1,), (1,)))
        res = res.astype(BF)
        for c in range(4):
            gls[n * 4 + c] = res[:, c * 128:(c + 1) * 128]
        return 0

    lax.fori_loop(0, 2, gl_step, 0)

    def gl_copy(n):
        c = (col + far(n)) % 8
        return link(gls.at[c], glr.at[n], gl_s.at[n], gl_r.at[n], (row, c))

    gl_cp = [Batch(7, gl_copy)]

    for cp in y_cp:
        cp.wait_recv()
    for c in range(8):
        acc = grs[mine, c].astype(F32) + gry[0, c].astype(F32) + gry[1, c].astype(F32)
        grz[c] = (acc + gry2[c // 4, c % 4].astype(F32)).astype(BF)
    slot = zl * 2 + ((y - y_src + 8) % 8) // 4

    def o_copy(n):
        return link(
            grz.at[n], gro.at[slot], o_s.at[n], o_r.at[slot], (8 * col + 2 * mine + k, n)
        )

    o_cp = [Batch(8, o_copy)]

    for cp in w1_cp + gl_cp + y_cp:
        cp.wait_send()
    for cp in w2_cp:
        cp.wait_recv()
    acc = wzb[0].astype(F32)
    for n in range(1, 8):
        acc = acc + wzb[n].astype(F32)
    wxb[x] = acc.astype(BF)
    w3_cp = [
        send(wxb.at[x], wxb.at[x], w3_s.at[d], w3_r.at[d], x_peers[d]) for d in range(3)
    ]
    for cp in w3_cp:
        cp.wait_recv()
    acc = wxb[0].astype(F32)
    for n in range(1, 4):
        acc = acc + wxb[n].astype(F32)
    wfin[k, first] = acc.astype(BF)

    def w4_copy(n):
        return link(wfin.at[k, first], wfin.at[k, first], w4_s.at[n], w4_r.at[n], first_peer(n))

    def w5_copy(n):
        piece = wfin.at[k, (first + 8 - far(n)) % 8]
        return link(piece, piece, w5_s.at[n + 1], w5_r.at[n + 1], twin)

    w4_cp = [Batch(7, w4_copy)]
    w5_cp = [send(wfin.at[k, first], wfin.at[k, first], w5_s.at[0], w5_r.at[0], twin)]

    for cp in gl_cp:
        cp.wait_recv()
    gl = gls[col].astype(F32)
    for d in range(7):
        gl = gl + glr[d].astype(F32)
    for n in range(8):
        wait_for(gro.at[n], o_s.at[n], o_r.at[n])
    gr = gro[0].astype(F32)
    for n in range(1, 8):
        gr = gr + gro[n].astype(F32)
    x0, x1 = gr[0:16], gr[16:32]
    ga = jnp.where(low, x0, pltpu.roll(x1, 64, 1))
    gb = jnp.where(low, pltpu.roll(x0, 64, 1), x1)
    gt = jnp.concatenate([gl, ga, gb, jnp.zeros((64, 128), F32)], axis=0).T
    hi = gt.astype(BF)
    rest = gt - hi.astype(F32)
    mid = rest.astype(BF)
    lo = (rest - mid.astype(F32)).astype(BF)
    wv = wcat[...]
    nt = ((1,), (0,))
    gn = f32dot(hi, wv, nt) + (f32dot(mid, wv, nt) + f32dot(lo, wv, nt))
    sc = scaled_v[...]
    mean_grad = jnp.mean(gn, axis=-1, keepdims=True)
    mean_cross = jnp.mean(gn * sc, axis=-1, keepdims=True)
    res = inv_v[...] * (gn - mean_grad - sc * mean_cross)
    sens[...] = res.astype(BF).reshape(2, 64, 256)
    s_cp = pltpu.make_async_copy(sens, sens_hbm, s_out.at[1])
    s_cp.start()
    for cp in o_cp + w2_cp + w3_cp:
        cp.wait_send()
    p_cp.wait()

    def forward(n, _):
        w4_copy(6 - n).wait_recv()
        w5_copy(6 - n).start()
        return 0

    lax.fori_loop(0, 7, forward, 0)
    w5_cp.append(Batch(7, w5_copy, start=False))
    for cp in w5_cp:
        cp.wait_recv()
    wg_cp = pltpu.make_async_copy(wfin, wfin_hbm, s_out.at[2])
    wg_cp.start()
    s_cp.wait()
    for cp in w4_cp + w5_cp:
        cp.wait_send()
    wg_cp.wait()


def hand_over(
    pair, sens, wfin, pair_out, sens_out, wg_out, pair_v, sens_v, wfin_v, wg_v, sem_in, sem_out
):
    trips = [(wfin, wfin_v), (sens, sens_v)]
    trips += [(pair.at[pl.ds(n, 2)], pair_v.at[pl.ds(n, 2)]) for n in range(0, 16, 2)]
    ins = [pltpu.make_async_copy(a, b, sem_in.at[n]) for n, (a, b) in enumerate(trips)]
    for cp in ins:
        cp.start()
    ins[0].wait()
    trips = [(wg_v.at[pl.ds(n, 256)], wg_out.at[pl.ds(n, 256)]) for n in range(0, 1024, 256)]
    trips += [(sens_v, sens_out)]
    trips += [(pair_v.at[pl.ds(n, 2)], pair_out.at[pl.ds(n, 2)]) for n in range(0, 16, 2)]
    outs = [pltpu.make_async_copy(a, b, sem_out.at[n]) for n, (a, b) in enumerate(trips)]
    for h in range(2):
        for n in range(8):
            blk = wfin_v[h, n].astype(F32) * (8.0 / 65536.0)
            for tt in range(2):
                wg_v[pl.ds(h * 16 + n * 2 + tt, 32, stride=32), :] = blk[tt * 32:(tt + 1) * 32]
    for cp in outs[:4]:
        cp.start()
    for a, b in zip(ins[1:], outs[4:]):
        a.wait()
        b.start()
    for cp in outs:
        cp.wait()


def on_device(acts, w1, w2, w, bias, g):
    anys = pl.BlockSpec(memory_space=pl.ANY)
    dma = pltpu.SemaphoreType.DMA
    scratch = [
        ((2, 64, 256), BF), ((1, 128), F32),
        ((128, 256), F32), ((128, 1), F32), ((128, 256), BF), ((1024, 128), BF), ((1024, 128), F32),
        ((32, 4096), BF), ((128, 2048), BF), ((8, 32, 128), BF), ((1024, 32), BF), ((32, 1024), BF),
        ((32, 128), BF), ((4, 2, 8, 32, 128), BF), ((2048, 128), F32), ((128, 2048), BF),
        ((2048, 128), BF),
        ((2048, 2048), BF), ((1024, 4096), BF), ((2, 16, 64, 128), BF), ((16, 64, 128), BF),
        ((1024, 128), F32), ((4, 8, 32, 128), BF), ((2, 8, 32, 128), BF), ((2, 4, 32, 128), BF),
        ((8, 32, 128), BF), ((8, 32, 128), BF), ((8, 32, 128), BF), ((7, 32, 128), BF),
        ((2, 512, 128), F32), ((2, 512, 128), BF), ((512, 128), BF), ((8, 64, 128), BF),
        ((7, 64, 128), BF), ((8, 64, 128), BF), ((4, 64, 128), BF), ((2, 8, 64, 128), BF),
        ((16, 128, 128), BF), ((2, 64, 256), BF),
    ]
    scratch = [pltpu.VMEM(s, d) for s, d in scratch]
    scratch += [dma((5,)), dma((16,)), dma((3,))]
    for n in (7, 8, 4, 5, 0, 4, 8, 7, 4, 7, 7, 3, 7, 8):
        scratch += [dma((n,)), dma((n,))] if n else [dma, dma]
    shapes = (
        jax.ShapeDtypeStruct((16, 128, 128), BF),
        jax.ShapeDtypeStruct((2, 64, 256), BF),
        jax.ShapeDtypeStruct((1024, 128), F32),
    )
    results = pl.pallas_call(
        kernel,
        out_shape=(*shapes[:2], jax.ShapeDtypeStruct((2, 8, 64, 128), BF)),
        in_specs=[anys] * 6,
        out_specs=(anys,) * 3,
        scratch_shapes=scratch,
        compiler_params=pltpu.CompilerParams(
            collective_id=0, has_side_effects=True, vmem_limit_bytes=64 * 2**20 - 65536
        ),
    )(acts, w1.T, w2.T, w, bias.reshape(1, 128), g)
    return pl.pallas_call(
        hand_over,
        out_shape=shapes,
        in_specs=[anys] * 3,
        out_specs=(anys,) * 3,
        scratch_shapes=[pltpu.VMEM(o.shape, o.dtype) for o in shapes[:2]]
        + [pltpu.VMEM((2, 8, 64, 128), BF), pltpu.VMEM((1024, 128), F32), dma((10,)), dma((13,))],
    )(*results)


def solution(mesh):
    return jax.shard_map(
        on_device,
        mesh=mesh,
        in_specs=(P(("row", "col"), None, None), P(), P(), P(), P(), P("row", "col", None)),
        out_specs=(P("row", "col", None), P(("row", "col"), None, None), P()),
        check_vma=False,
    )
```
